128 devices in a mesh: fsdp: 64 (over x, z, y_hi, core), mat: 2 (over y_lo).
Axes of the slice: x: 4, y: 4 (y_hi: 2, y_lo: 2; y = y_hi * 2 + y_lo), z: 4, core: 2. Of those that a mesh axis runs over, the one named last changes fastest.
Arguments:
- gradient: bfloat16 [8192, 14336], P('fsdp', 'mat'), may hold values from -40000 to 40000, as said below
- weight: bfloat16 [8192, 14336], P('fsdp', 'mat'), may hold values from -6 to 6
- projector: bfloat16 [8192, 768], P('fsdp'), may hold values from -0.0625 to 0.0625
- first_moment: float32 [768, 14336], P('fsdp', 'mat'), may hold values from -6 to 6
- second_moment: float32 [768, 14336], P('fsdp', 'mat'), may hold values from 0.25 to 4
Outputs:
- new_weight: bfloat16 [8192, 14336], P('fsdp', 'mat')
- new_first: float32 [768, 14336], P('fsdp', 'mat')
- new_second: float32 [768, 14336], P('fsdp', 'mat')
The draws below stay inside these ranges and needn't reach their ends.
Inputs may be any that keep to these rules, and one draw needn't show every extreme that they name: gradient entries are finite and not all zero.
All inputs are finite; a program needn't handle non-finite values.
Results may differ from the reference program's by a relative error of at most 0.0017.
Values may be sent and summed in bfloat16 or wider, within the bound.
A program may use at most 128 MiB of HBM per device.

```python
import math
import jax
import jax.numpy as jnp

D = 8192
FW = 14336
R = 768


def draw_gradient(key, part):
    key = jax.random.fold_in(key, 11)
    key_base, key_rows, key_cols = jax.random.split(key, 3)
    row_pos = jnp.arange(D, dtype=jnp.float32) / (D - 1)
    col_pos = jnp.arange(FW, dtype=jnp.float32) / (FW - 1)
    rise = 3.0
    base = jnp.clip(jax.random.normal(key_base, (D, FW), jnp.float32), -4.0, 4.0)
    row_scale = jnp.exp(jnp.log(rise) * row_pos + jnp.log(10.0) * jax.random.uniform(key_rows, (D,), jnp.float32))
    col_scale = jnp.exp(jnp.log(rise) * col_pos + jnp.log(10.0) * jax.random.uniform(key_cols, (FW,), jnp.float32))
    return (base * row_scale[:, None] * col_scale[None, :]).astype(jnp.bfloat16)


def levels(own_key, shape, shards, low, high):
    def one(axis_at, shards_of):
        steps = jax.random.uniform(jax.random.fold_in(jax.random.fold_in(own_key, 6), axis_at), (shards_of,), jnp.float32, low / len(shards), high / len(shards))
        return jnp.repeat(jnp.exp(steps), shape[axis_at] // shards_of).reshape((-1,) + (1,) * (len(shape) - axis_at - 1))

    gain = one(*shards[0])
    for cut in shards[1:]:
        gain = gain * one(*cut)
    return gain


def normal_values(own_key, dims, width, bound, cuts=(), held_as=jnp.bfloat16):
    entries = width * jax.random.normal(own_key, dims, jnp.float32)
    if cuts:
        entries = entries * levels(own_key, dims, cuts, -0.22, 0.18)
    return jnp.clip(entries, -bound, bound).astype(held_as)


def setup_inputs(seed: int = 0) -> dict:
    key_list = jax.random.split(jax.random.key(seed), 6)
    gradient = draw_gradient(jax.random.fold_in(key_list[5], 71), 0)
    weight = normal_values(key_list[1], (D, FW), 1.0, 6.0, ((0, 64), (1, 2)))
    projector = normal_values(key_list[2], (D, R), D ** -0.5, 0.0625, ((0, 64),))
    first_moment = normal_values(key_list[3], (R, FW), 1.0, 6.0, ((0, 64), (1, 2)), jnp.float32)
    second_moment = jnp.clip(jnp.exp(math.log(4.0) - 2.7725887 * jax.random.uniform(key_list[4], (R, FW), jnp.float32) ** levels(key_list[4], (R, FW), ((0, 64), (1, 2)), -0.2, 0.2)), 0.25, 4.0)
    return dict(gradient=gradient, weight=weight, projector=projector, first_moment=first_moment, second_moment=second_moment)


def reference(gradient, weight, projector, first_moment, second_moment):
    wide = gradient.astype(jnp.float32)
    squares = jnp.sum(wide * wide)
    clip = jnp.minimum(1.0, 1.0 / jnp.sqrt(squares / (D * FW) + 1e-06))
    low = jnp.dot(projector.T, gradient, preferred_element_type=jnp.float32)
    scaled = clip * low
    new_first = 0.9 * first_moment + 0.1 * scaled
    new_second = 0.95 * second_moment + 0.05 * scaled * scaled
    direction = (new_first / (jnp.sqrt(new_second) + 1e-08)).astype(jnp.bfloat16)
    update = jnp.dot(projector, direction, preferred_element_type=jnp.float32)
    new_weight = (weight.astype(jnp.float32) - 0.25 * update).astype(jnp.bfloat16)
    return (new_weight, new_first, new_second)
```

```python
import functools

import jax
import jax.numpy as jnp
from jax import lax
from jax.experimental import pallas as pl
from jax.experimental.pallas import tpu as pltpu
from jax.sharding import PartitionSpec as P

D = 8192
FW = 14336
R = 768
ROWS = 128
COLS = 7168
HALF = COLS // 2
OWN = HALF // 4
MR = 12
CHUNKS = ((0, 512), (512, 384))
K = len(CHUNKS)
MESH = pl.DeviceIdType.MESH
BF = jnp.bfloat16
F32 = jnp.float32
NT = (((1,), (1,)), ((), ()))


def kernel(
    g_ref, w_ref, p_ref, m1_ref, m2_ref,
    nw_ref, n1_ref, n2_ref,
    gl, wl, pl_, g_all, pt, pn, own, cs, cr, zs, zr, fin, ys, yr, mi, mo, df, dr, us, ur, sq, sqr,
    lsem, msem, osem,
    g_s, g_r, p_s, p_r, mi_s, mi_r, c_s, c_r, z_s, z_r, y_s, y_r,
    dy_s, dy_r, dz_s, dz_r, dc_s, dc_r, mo_s, mo_r, u_s, u_r, q_s, q_r,
):
    f = lax.axis_index("fsdp")
    yl = lax.axis_index("mat")
    c = lax.rem(f, 2)
    yh = lax.rem(lax.div(f, 2), 2)
    z = lax.rem(lax.div(f, 4), 4)
    x = lax.div(f, 16)

    def dev(x_, z_, yh_, yl_, c_):
        return (((x_ * 4 + z_) * 2 + yh_) * 2 + c_, yl_)

    def along_x(d):
        return dev(lax.rem(x + d, 4), z, yh, yl, c)

    def along_z(d):
        return dev(x, lax.rem(z + d, 4), yh, yl, c)

    def along_y(d):
        t = lax.rem(yh * 2 + yl + d, 4)
        return dev(x, z, lax.div(t, 2), lax.rem(t, 2), c)

    mate = dev(x, z, yh, yl, 1 - c)
    across = dev(x, z, 1 - yh, yl, c)
    grp = (along_x, along_z)
    red = (along_z, along_x)
    gq = (x, z)
    rq = (z, x)

    def rows(start, size, of):
        return pl.ds(pl.multiple_of(start, of), size)

    def at_cols(h, j, k):
        return rows(h * HALF + j * OWN + CHUNKS[k][0], CHUNKS[k][1], 128)

    def remote(src, dst, s, r, to):
        return pltpu.make_async_remote_copy(
            src_ref=src, dst_ref=dst, send_sem=s, recv_sem=r, device_id=to, device_id_type=MESH
        )

    load_p = pltpu.make_async_copy(p_ref, pl_, lsem.at[0])
    load_g = pltpu.make_async_copy(g_ref, gl, lsem.at[1])
    load_w = pltpu.make_async_copy(w_ref, wl, lsem.at[2])
    load_p.start()
    load_g.start()
    load_w.start()

    barrier = pltpu.get_barrier_semaphore()
    partners = [mate] + [a(d) for a in (along_x, along_z, along_y) for d in (1, 2, 3)]
    for to in partners:
        pl.semaphore_signal(barrier, inc=1, device_id=to, device_id_type=MESH)

    load_p.wait()
    for h in range(2):
        for b in range(R // 128):
            i = lax.broadcasted_iota(jnp.int32, (128, 128), 0) + b * 128
            t = lax.rem(i, MR)
            i = lax.div(i, MR)
            j = lax.rem(i, 4)
            i = lax.div(i, 4)
            yh_ = lax.rem(i, 2)
            i = lax.div(i, 2)
            r_ = lax.rem(i, 4)
            c_ = lax.div(i, 4)
            x_, z_ = (j, r_) if h == 0 else (r_, j)
            want = (((x_ * 4 + z_) * 2 + yh_) * 2 + c_) * MR + t
            lane = lax.broadcasted_iota(jnp.int32, (128, 128), 1)
            one = jnp.concatenate(
                [jnp.where(want == lane + n * 128, 1.0, 0.0).astype(BF) for n in range(R // 128)], axis=1
            )
            pt[h, b * 128 : (b + 1) * 128, rows(gq[h] * ROWS, ROWS, ROWS)] = lax.dot_general(
                one, pl_[...], NT, preferred_element_type=F32
            ).astype(BF)

    pl.semaphore_wait(barrier, len(partners))

    def p_copy(h, d):
        mine = pt.at[h, :, rows(gq[h] * ROWS, ROWS, ROWS)]
        return remote(mine, mine, p_s.at[h, d - 1], p_r.at[h, d - 1], grp[h](d))

    def g_copy(h, k, d):
        j = lax.rem(gq[h] + d, 4)
        off, n = CHUNKS[k]
        return remote(
            g_ref.at[:, at_cols(h, j, k)],
            g_all.at[h, rows(gq[h] * ROWS, ROWS, ROWS), pl.ds(off, n)],
            g_s.at[h, k, d - 1], g_r.at[h, k, d - 1], grp[h](d),
        )

    def g_own(h):
        return pltpu.make_async_copy(
            g_ref.at[:, rows(h * HALF + gq[h] * OWN, OWN, 128)],
            g_all.at[h, rows(gq[h] * ROWS, ROWS, ROWS), :],
            lsem.at[3 + h],
        )

    def mi_copy(h, m, d):
        j = lax.rem(gq[h] + d, 4)
        return remote(
            (m1_ref, m2_ref)[m].at[:, rows(h * HALF + j * OWN, OWN, 128)],
            mi.at[h, m, gq[h]],
            mi_s.at[h, m, d - 1], mi_r.at[h, m, d - 1], grp[h](d),
        )

    def mi_own(h, m):
        return pltpu.make_async_copy(
            (m1_ref, m2_ref)[m].at[:, rows(h * HALF + gq[h] * OWN, OWN, 128)], mi.at[h, m, gq[h]], msem.at[h, m]
        )

    order = (2, 1, 3)
    for d in order:
        for h in range(2):
            p_copy(h, d).start()
    for k in range(K):
        for d in order:
            for h in range(2):
                g_copy(h, k, d).start()
    for h in range(2):
        g_own(h).start()
        for m in range(2):
            mi_own(h, m).start()
    for d in order:
        for h in range(2):
            for m in range(2):
                mi_copy(h, m, d).start()

    load_g.wait()

    def add_squares(i, total):
        block = gl[rows(i * 16, 16, 16), :].astype(F32)
        block = block * block
        for n in range(COLS // 1024):
            part = block[:, n * 1024 : (n + 1) * 1024]
            total = total + part
        return total

    total = lax.fori_loop(0, ROWS // 16, add_squares, jnp.zeros((16, 1024), F32))
    total = total[:8] + total[8:]
    part = total[:, :128]
    for n in range(1, 8):
        part = part + total[:, n * 128 : (n + 1) * 128]
    at = 0
    for stage, to in enumerate(([mate], *([a(d) for d in (1, 2, 3)] for a in (along_x, along_z, along_y)))):
        sq[stage] = part
        copies = [
            remote(sq.at[stage], sqr.at[at + n], q_s.at[at + n], q_r.at[at + n], who) for n, who in enumerate(to)
        ]
        for copy in copies:
            copy.start()
        for copy in copies:
            copy.wait()
        for n in range(len(to)):
            part = part + sqr[at + n]
        at += len(to)
    squares = jnp.sum(jnp.sum(part, axis=1, keepdims=True), axis=0, keepdims=True)
    clip = jnp.minimum(1.0, 1.0 / jnp.sqrt(squares / (D * FW) + 1e-06))

    def c_copy(h, k):
        cols = pl.ds(*CHUNKS[k])
        return remote(cs.at[h, :, cols], cr.at[h, :, cols], c_s.at[h, k], c_r.at[h, k], mate)

    def z_copy(h, k, d):
        cols = pl.ds(*CHUNKS[k])
        to = lax.rem(rq[h] + d, 4)
        return remote(
            zs.at[h, rows(to * 96, 96, 96), cols], zr.at[h, d - 1, :, cols],
            z_s.at[h, k, d - 1], z_r.at[h, k, d - 1], red[h](d),
        )

    def y_copy(h, k):
        cols = pl.ds(*CHUNKS[k])
        return remote(ys.at[h, :, cols], yr.at[h, :, cols], y_s.at[h, k], y_r.at[h, k], across)

    def dr_rows(h, yh_):
        return rows(c * 384 + rq[h] * 96 + yh_ * 48, 48, 48)

    def dy_copy(h, k):
        mine = dr.at[h, dr_rows(h, yh), pl.ds(*CHUNKS[k])]
        return remote(mine, mine, dy_s.at[h, k], dy_r.at[h, k], across)

    def dz_copy(h, k, e, d):
        mine = dr.at[h, dr_rows(h, yh if e == 0 else 1 - yh), pl.ds(*CHUNKS[k])]
        return remote(mine, mine, dz_s.at[h, k, e, d - 1], dz_r.at[h, k, e, d - 1], red[h](d))

    def dc_copy(h, k):
        mine = dr.at[h, rows(c * 384, 384, 384), pl.ds(*CHUNKS[k])]
        return remote(mine, mine, dc_s.at[h, k], dc_r.at[h, k], mate)

    def mo_copy(h, k, m, d):
        j = lax.rem(gq[h] + d, 4)
        return remote(
            mo.at[h, m, j, :, pl.ds(*CHUNKS[k])], (n1_ref, n2_ref)[m].at[:, at_cols(h, gq[h], k)],
            mo_s.at[h, k, m, d - 1], mo_r.at[h, k, m, d - 1], grp[h](d),
        )

    def mo_own(h, k, m):
        return pltpu.make_async_copy(
            mo.at[h, m, gq[h], :, pl.ds(*CHUNKS[k])], (n1_ref, n2_ref)[m].at[:, at_cols(h, gq[h], k)],
            osem.at[h, k, m],
        )

    def u_copy(h, k, d):
        j = lax.rem(gq[h] + d, 4)
        return remote(
            us.at[h, rows(j * ROWS, ROWS, ROWS), pl.ds(*CHUNKS[k])], ur.at[:, at_cols(h, gq[h], k)],
            u_s.at[h, k, d - 1], u_r.at[h, k, d - 1], grp[h](d),
        )

    def nw_copy(h, k, j):
        return pltpu.make_async_copy(
            wl.at[:, at_cols(h, j, k)], nw_ref.at[:, at_cols(h, j, k)], osem.at[h, k, 2]
        )

    def multiply(k):
        off, n = CHUNKS[k]
        cols = slice(off, off + n)
        for h in range(2):
            if k == 0:
                g_own(h).wait()
                for d in order:
                    p_copy(h, d).wait()
            for d in order:
                g_copy(h, k, d).wait()
            for b in range(3):
                cs[h, b * 128 : (b + 1) * 128, cols] = jnp.dot(
                    pt[h, rows((1 - c) * 384 + b * 128, 128, 128), :], g_all[h, :, cols], preferred_element_type=F32
                ).astype(BF)
            c_copy(h, k).start()
        for h in range(2):
            for b in range(3):
                own[h, b * 128 : (b + 1) * 128, cols] = jnp.dot(
                    pt[h, rows(c * 384 + b * 128, 128, 128), :], g_all[h, :, cols], preferred_element_type=F32
                )

    def add_core(k):
        off, n = CHUNKS[k]
        cols = slice(off, off + n)
        for h in range(2):
            c_copy(h, k).wait()
            for d in order:
                part = rows(lax.rem(rq[h] + d, 4) * 96, 96, 96)
                zs[h, part, cols] = (own[h, part, cols] + cr[h, part, cols].astype(F32)).astype(BF)
                z_copy(h, k, d).start()

    def add_ring(k):
        off, n = CHUNKS[k]
        cols = slice(off, off + n)
        for h in range(2):
            for d in order:
                z_copy(h, k, d).wait()

            def total(yh_):
                part = rows(rq[h] * 96 + yh_ * 48, 48, 48)
                sum_ = own[h, part, cols] + cr[h, part, cols].astype(F32)
                for e in range(3):
                    sum_ = sum_ + zr[h, e, rows(yh_ * 48, 48, 48), cols].astype(F32)
                return sum_

            ys[h, :, cols] = total(1 - yh).astype(BF)
            y_copy(h, k).start()
            fin[h, :, cols] = total(yh)

    def adam(k):
        off, n = CHUNKS[k]
        cols = slice(off, off + n)
        for h in range(2):
            if k == 0:
                for m in range(2):
                    mi_own(h, m).wait()
                    for d in order:
                        mi_copy(h, m, d).wait()
            y_copy(h, k).wait()
            fin[h, :, cols] = fin[h, :, cols] + yr[h, :, cols].astype(F32)
            for j in range(4):
                scaled = clip * fin[h, j * MR : (j + 1) * MR, cols]
                first = 0.9 * mi[h, 0, j, :, cols] + 0.1 * scaled
                second = 0.95 * mi[h, 1, j, :, cols] + 0.05 * scaled * scaled
                mo[h, 0, j, :, cols] = first
                mo[h, 1, j, :, cols] = second
                df[h, j * MR : (j + 1) * MR, cols] = first / (jnp.sqrt(second) + 1e-08)
            dr[h, dr_rows(h, yh), cols] = df[h, :, cols].astype(BF)
            dy_copy(h, k).start()
            for d in order:
                dz_copy(h, k, 0, d).start()
        for h in range(2):
            for m in range(2):
                mo_own(h, k, m).start()
                for d in order:
                    mo_copy(h, k, m, d).start()

    def spread(k):
        for h in range(2):
            dy_copy(h, k).wait()
            for d in order:
                dz_copy(h, k, 1, d).start()

    def share(k):
        for h in range(2):
            for e in range(2):
                for d in order:
                    dz_copy(h, k, e, d).wait()
            dc_copy(h, k).start()

    def transpose_projector():
        for h in range(2):
            for b in range(R // 128):
                i = lax.broadcasted_iota(jnp.int32, (512, 512), 0)
                eye = (i == lax.broadcasted_iota(jnp.int32, (512, 512), 1)).astype(F32).astype(BF)
                pn[h, :, b * 128 : (b + 1) * 128] = lax.dot_general(
                    eye, pt[h, b * 128 : (b + 1) * 128, :], NT, preferred_element_type=F32
                ).astype(BF)

    def update(k):
        off, n = CHUNKS[k]
        cols = slice(off, off + n)
        for h in range(2):
            dc_copy(h, k).wait()
            for d in (2, 1, 3, 0):
                part = rows(lax.rem(gq[h] + d, 4) * ROWS, ROWS, ROWS)
                us[h, part, cols] = jnp.dot(pn[h, part, :], dr[h, :, cols], preferred_element_type=F32).astype(BF)
                if d:
                    u_copy(h, k, d).start()

    def weight(k):
        off, n = CHUNKS[k]
        cols = slice(off, off + n)
        for h in range(2):
            for d in (0, 1, 3, 2):
                j = lax.rem(gq[h] - d + 4, 4)
                here = at_cols(h, j, k)
                if d:
                    u_copy(h, k, d).wait()
                    u = ur[:, here]
                else:
                    u = us[h, rows(gq[h] * ROWS, ROWS, ROWS), cols]
                wl[:, here] = (wl[:, here].astype(F32) - 0.25 * u.astype(F32)).astype(BF)

    last = K + 7
    for step in range(last):
        for s, run in reversed(list(enumerate((multiply, add_core, add_ring, adam, spread, share, update)))):
            if 0 <= step - s < K:
                run(step - s)
        if step == 1:
            transpose_projector()
    load_w.wait()
    for k in range(K):
        weight(k)
    out = pltpu.make_async_copy(wl, nw_ref, lsem.at[5])
    out.start()
    for k in range(K):
        for h in range(2):
            for m in range(2):
                mo_own(h, k, m).wait()
                for d in order:
                    mo_copy(h, k, m, d).wait()
    out.wait()


def shards(gradient, weight, projector, first_moment, second_moment):
    dma = pltpu.SemaphoreType.DMA
    hk = dma((2, K))
    hkd = dma((2, K, 3))
    return pl.pallas_call(
        kernel,
        out_shape=(
            jax.ShapeDtypeStruct((ROWS, COLS), BF),
            jax.ShapeDtypeStruct((MR, COLS), F32),
            jax.ShapeDtypeStruct((MR, COLS), F32),
        ),
        in_specs=[pl.BlockSpec(memory_space=pl.ANY)] * 5,
        out_specs=[pl.BlockSpec(memory_space=pl.ANY)] * 3,
        scratch_shapes=[
            pltpu.VMEM((ROWS, COLS), BF),
            pltpu.VMEM((ROWS, COLS), BF),
            pltpu.VMEM((ROWS, R), BF),
            pltpu.VMEM((2, 512, OWN), BF),
            pltpu.VMEM((2, R, 512), BF),
            pltpu.VMEM((2, 512, R), BF),
            pltpu.VMEM((2, 384, OWN), F32),
            pltpu.VMEM((2, 384, OWN), BF),
            pltpu.VMEM((2, 384, OWN), BF),
            pltpu.VMEM((2, 384, OWN), BF),
            pltpu.VMEM((2, 3, 96, OWN), BF),
            pltpu.VMEM((2, 48, OWN), F32),
            pltpu.VMEM((2, 48, OWN), BF),
            pltpu.VMEM((2, 48, OWN), BF),
            pltpu.VMEM((2, 2, 4, MR, OWN), F32),
            pltpu.VMEM((2, 2, 4, MR, OWN), F32),
            pltpu.VMEM((2, 48, OWN), F32),
            pltpu.VMEM((2, R, OWN), BF),
            pltpu.VMEM((2, 512, OWN), BF),
            pltpu.VMEM((ROWS, COLS), BF),
            pltpu.VMEM((4, 8, 128), F32),
            pltpu.VMEM((10, 8, 128), F32),
            dma((6,)), dma((2, 2)), dma((2, K, 3)),
            hkd, hkd,
            dma((2, 3)), dma((2, 3)),
            dma((2, 2, 3)), dma((2, 2, 3)),
            hk, hk,
            hkd, hkd,
            hk, hk,
            hk, hk,
            dma((2, K, 2, 3)), dma((2, K, 2, 3)),
            hk, hk,
            dma((2, K, 2, 3)), dma((2, K, 2, 3)),
            hkd, hkd,
            dma((10,)), dma((10,)),
        ],
        compiler_params=pltpu.CompilerParams(
            collective_id=0, has_side_effects=True, vmem_limit_bytes=50 * 1024 * 1024
        ),
        cost_estimate=pl.CostEstimate(flops=4 * ROWS * R * COLS, bytes_accessed=7_000_000, transcendentals=86016),
    )(gradient, weight, projector, first_moment, second_moment)


def solution(mesh):
    split = P("fsdp", "mat")
    return jax.shard_map(
        shards,
        mesh=mesh,
        in_specs=(split, split, P("fsdp", None), split, split),
        out_specs=(split, split, split),
        check_vma=False,
    )
```

```python
import functools

import jax
import jax.numpy as jnp
from jax import lax
from jax.experimental import pallas as pl
from jax.experimental.pallas import tpu as pltpu
from jax.sharding import PartitionSpec as P

D = 8192
FW = 14336
R = 768
ROWS = 128
COLS = 7168
HALF = COLS // 2
OWN = HALF // 4
MR = 12
CHUNKS = ((0, 512), (512, 384))
K = len(CHUNKS)
MESH = pl.DeviceIdType.MESH
BF = jnp.bfloat16
F32 = jnp.float32
NT = (((1,), (1,)), ((), ()))


def kernel(
    g_ref, w_ref, p_ref, m1_ref, m2_ref,
    nw_ref, n1_ref, n2_ref,
    gl, wl, pl_, g_all, pt, pn, own, cs, cr, zs, zr, fin, ys, yr, mi, mo, df, dr, us, ur, sq, sqr, scale,
    lsem, msem, osem,
    g_s, g_r, p_s, p_r, mi_s, mi_r, c_s, c_r, z_s, z_r, y_s, y_r,
    dy_s, dy_r, dz_s, dz_r, dc_s, dc_r, mo_s, mo_r, u_s, u_r, q_s, q_r,
):
    f = lax.axis_index("fsdp")
    yl = lax.axis_index("mat")
    c = lax.rem(f, 2)
    yh = lax.rem(lax.div(f, 2), 2)
    z = lax.rem(lax.div(f, 4), 4)
    x = lax.div(f, 16)

    def dev(x_, z_, yh_, yl_, c_):
        return (((x_ * 4 + z_) * 2 + yh_) * 2 + c_, yl_)

    def along_x(d):
        return dev(lax.rem(x + d, 4), z, yh, yl, c)

    def along_z(d):
        return dev(x, lax.rem(z + d, 4), yh, yl, c)

    def along_y(d):
        t = lax.rem(yh * 2 + yl + d, 4)
        return dev(x, z, lax.div(t, 2), lax.rem(t, 2), c)

    mate = dev(x, z, yh, yl, 1 - c)
    across = dev(x, z, 1 - yh, yl, c)
    grp = (along_x, along_z)
    red = (along_z, along_x)
    gq = (x, z)
    rq = (z, x)

    def rows(start, size, of):
        return pl.ds(pl.multiple_of(start, of), size)

    def at_cols(h, j, k):
        return rows(h * HALF + j * OWN + CHUNKS[k][0], CHUNKS[k][1], 128)

    def remote(src, dst, s, r, to):
        return pltpu.make_async_remote_copy(
            src_ref=src, dst_ref=dst, send_sem=s, recv_sem=r, device_id=to, device_id_type=MESH
        )

    load_p = pltpu.make_async_copy(p_ref, pl_, lsem.at[0])
    load_g = pltpu.make_async_copy(g_ref, gl, lsem.at[1])
    load_w = pltpu.make_async_copy(w_ref, wl, lsem.at[2])
    load_p.start()
    load_g.start()
    load_w.start()

    barrier = pltpu.get_barrier_semaphore()
    partners = [mate] + [a(d) for a in (along_x, along_z, along_y) for d in (1, 2, 3)]
    for to in partners:
        pl.semaphore_signal(barrier, inc=1, device_id=to, device_id_type=MESH)

    load_p.wait()
    for h in range(2):
        for b in range(R // 128):
            i = lax.broadcasted_iota(jnp.int32, (128, 128), 0) + b * 128
            t = lax.rem(i, MR)
            i = lax.div(i, MR)
            j = lax.rem(i, 4)
            i = lax.div(i, 4)
            yh_ = lax.rem(i, 2)
            i = lax.div(i, 2)
            r_ = lax.rem(i, 4)
            c_ = lax.div(i, 4)
            x_, z_ = (j, r_) if h == 0 else (r_, j)
            want = (((x_ * 4 + z_) * 2 + yh_) * 2 + c_) * MR + t
            lane = lax.broadcasted_iota(jnp.int32, (128, 128), 1)
            one = jnp.concatenate(
                [jnp.where(want == lane + n * 128, 1.0, 0.0).astype(BF) for n in range(R // 128)], axis=1
            )
            pt[h, b * 128 : (b + 1) * 128, rows(gq[h] * ROWS, ROWS, ROWS)] = lax.dot_general(
                one, pl_[...], NT, preferred_element_type=F32
            ).astype(BF)

    pl.semaphore_wait(barrier, len(partners))

    def p_copy(h, d):
        mine = pt.at[h, :, rows(gq[h] * ROWS, ROWS, ROWS)]
        return remote(mine, mine, p_s.at[h, d - 1], p_r.at[h, d - 1], grp[h](d))

    def g_copy(h, k, d):
        j = lax.rem(gq[h] + d, 4)
        off, n = CHUNKS[k]
        return remote(
            g_ref.at[:, at_cols(h, j, k)],
            g_all.at[h, rows(gq[h] * ROWS, ROWS, ROWS), pl.ds(off, n)],
            g_s.at[h, k, d - 1], g_r.at[h, k, d - 1], grp[h](d),
        )

    def g_own(h):
        return pltpu.make_async_copy(
            g_ref.at[:, rows(h * HALF + gq[h] * OWN, OWN, 128)],
            g_all.at[h, rows(gq[h] * ROWS, ROWS, ROWS), :],
            lsem.at[3 + h],
        )

    def mi_copy(h, m, d):
        j = lax.rem(gq[h] + d, 4)
        return remote(
            (m1_ref, m2_ref)[m].at[:, rows(h * HALF + j * OWN, OWN, 128)],
            mi.at[h, m, gq[h]],
            mi_s.at[h, m, d - 1], mi_r.at[h, m, d - 1], grp[h](d),
        )

    def mi_own(h, m):
        return pltpu.make_async_copy(
            (m1_ref, m2_ref)[m].at[:, rows(h * HALF + gq[h] * OWN, OWN, 128)], mi.at[h, m, gq[h]], msem.at[h, m]
        )

    order = (2, 1, 3)
    for d in order:
        for h in range(2):
            p_copy(h, d).start()
    for k in range(K):
        for d in order:
            for h in range(2):
                g_copy(h, k, d).start()
    for h in range(2):
        g_own(h).start()
        for m in range(2):
            mi_own(h, m).start()
    load_g.wait()

    def add_squares(i, total):
        block = gl[rows(i * 16, 16, 16), :].astype(F32)
        block = block * block
        for n in range(COLS // 1024):
            part = block[:, n * 1024 : (n + 1) * 1024]
            total = total + part
        return total

    total = lax.fori_loop(0, ROWS // 16, add_squares, jnp.zeros((16, 1024), F32))
    total = total[:8] + total[8:]
    part = total[:, :128]
    for n in range(1, 8):
        part = part + total[:, n * 128 : (n + 1) * 128]
    def sq_copies(stage):
        to = ([mate], *([a(d) for d in (1, 2, 3)] for a in (along_y, along_x, along_z)))[stage]
        at = (0, 1, 4, 7)[stage]
        return [remote(sq.at[stage], sqr.at[at + n], q_s.at[at + n], q_r.at[at + n], who) for n, who in enumerate(to)]

    def sq_start(stage):
        for copy in sq_copies(stage):
            copy.start()

    def sq_done(stage):
        copies = sq_copies(stage)
        at = (0, 1, 4, 7)[stage]
        for copy in copies:
            copy.wait()
        part = sq[stage]
        for n in range(len(copies)):
            part = part + sqr[at + n]
        if stage < 3:
            sq[stage + 1] = part
            sq_start(stage + 1)
        return part

    sq[0] = part
    sq_start(0)
    sq_done(0)
    sq_done(1)

    def clip_of(part):
        squares = jnp.sum(jnp.sum(part, axis=1, keepdims=True), axis=0, keepdims=True)
        return jnp.minimum(1.0, 1.0 / jnp.sqrt(squares / (D * FW) + 1e-06))

    def c_copy(h, k):
        cols = pl.ds(*CHUNKS[k])
        return remote(cs.at[h, :, cols], cr.at[h, :, cols], c_s.at[h, k], c_r.at[h, k], mate)

    def z_copy(h, k, d):
        cols = pl.ds(*CHUNKS[k])
        to = lax.rem(rq[h] + d, 4)
        return remote(
            zs.at[h, rows(to * 96, 96, 96), cols], zr.at[h, d - 1, :, cols],
            z_s.at[h, k, d - 1], z_r.at[h, k, d - 1], red[h](d),
        )

    def y_copy(h, k):
        cols = pl.ds(*CHUNKS[k])
        return remote(ys.at[h, :, cols], yr.at[h, :, cols], y_s.at[h, k], y_r.at[h, k], across)

    def dr_rows(h, yh_):
        return rows(c * 384 + rq[h] * 96 + yh_ * 48, 48, 48)

    def dy_copy(h, k):
        mine = dr.at[h, dr_rows(h, yh), pl.ds(*CHUNKS[k])]
        return remote(mine, mine, dy_s.at[h, k], dy_r.at[h, k], across)

    def dz_copy(h, k, e, d):
        mine = dr.at[h, dr_rows(h, yh if e == 0 else 1 - yh), pl.ds(*CHUNKS[k])]
        return remote(mine, mine, dz_s.at[h, k, e, d - 1], dz_r.at[h, k, e, d - 1], red[h](d))

    def dc_copy(h, k):
        mine = dr.at[h, rows(c * 384, 384, 384), pl.ds(*CHUNKS[k])]
        return remote(mine, mine, dc_s.at[h, k], dc_r.at[h, k], mate)

    def mo_copy(h, k, m, d):
        j = lax.rem(gq[h] + d, 4)
        return remote(
            mo.at[h, m, j, :, pl.ds(*CHUNKS[k])], (n1_ref, n2_ref)[m].at[:, at_cols(h, gq[h], k)],
            mo_s.at[h, k, m, d - 1], mo_r.at[h, k, m, d - 1], grp[h](d),
        )

    def mo_own(h, k, m):
        return pltpu.make_async_copy(
            mo.at[h, m, gq[h], :, pl.ds(*CHUNKS[k])], (n1_ref, n2_ref)[m].at[:, at_cols(h, gq[h], k)],
            osem.at[h, k, m],
        )

    def u_copy(h, k, d):
        j = lax.rem(gq[h] + d, 4)
        return remote(
            us.at[h, rows(j * ROWS, ROWS, ROWS), pl.ds(*CHUNKS[k])], ur.at[:, at_cols(h, gq[h], k)],
            u_s.at[h, k, d - 1], u_r.at[h, k, d - 1], grp[h](d),
        )

    def multiply(k):
        off, n = CHUNKS[k]
        cols = slice(off, off + n)
        for h in range(2):
            if k == 0:
                g_own(h).wait()
                for d in order:
                    p_copy(h, d).wait()
            for d in order:
                g_copy(h, k, d).wait()
            for b in range(3):
                cs[h, b * 128 : (b + 1) * 128, cols] = jnp.dot(
                    pt[h, rows((1 - c) * 384 + b * 128, 128, 128), :], g_all[h, :, cols], preferred_element_type=F32
                ).astype(BF)
            c_copy(h, k).start()
        for h in range(2):
            for b in range(3):
                own[h, b * 128 : (b + 1) * 128, cols] = jnp.dot(
                    pt[h, rows(c * 384 + b * 128, 128, 128), :], g_all[h, :, cols], preferred_element_type=F32
                )

    def add_core(k):
        off, n = CHUNKS[k]
        cols = slice(off, off + n)
        for h in range(2):
            c_copy(h, k).wait()
            for d in order:
                part = rows(lax.rem(rq[h] + d, 4) * 96, 96, 96)
                zs[h, part, cols] = (own[h, part, cols] + cr[h, part, cols].astype(F32)).astype(BF)
                z_copy(h, k, d).start()
        if k == 0:
            for d in order:
                for h in range(2):
                    for m in range(2):
                        mi_copy(h, m, d).start()

    def add_ring(k):
        off, n = CHUNKS[k]
        cols = slice(off, off + n)
        if k == 0:
            sq_done(2)
        for h in range(2):
            for d in order:
                z_copy(h, k, d).wait()

            def total(yh_):
                part = rows(rq[h] * 96 + yh_ * 48, 48, 48)
                sum_ = own[h, part, cols] + cr[h, part, cols].astype(F32)
                for e in range(3):
                    sum_ = sum_ + zr[h, e, rows(yh_ * 48, 48, 48), cols].astype(F32)
                return sum_

            ys[h, :, cols] = total(1 - yh).astype(BF)
            y_copy(h, k).start()
            fin[h, :, cols] = total(yh)

    def adam(k):
        off, n = CHUNKS[k]
        cols = slice(off, off + n)
        if k == 0:
            scale[...] = jnp.broadcast_to(clip_of(sq_done(3)), (8, 128))
        clip = scale[:1, :1]
        for h in range(2):
            if k == 0:
                for m in range(2):
                    mi_own(h, m).wait()
                    for d in order:
                        mi_copy(h, m, d).wait()
            y_copy(h, k).wait()
            fin[h, :, cols] = fin[h, :, cols] + yr[h, :, cols].astype(F32)
            for j in range(4):
                scaled = clip * fin[h, j * MR : (j + 1) * MR, cols]
                first = 0.9 * mi[h, 0, j, :, cols] + 0.1 * scaled
                second = 0.95 * mi[h, 1, j, :, cols] + 0.05 * scaled * scaled
                mo[h, 0, j, :, cols] = first
                mo[h, 1, j, :, cols] = second
                df[h, j * MR : (j + 1) * MR, cols] = first / (jnp.sqrt(second) + 1e-08)
            dr[h, dr_rows(h, yh), cols] = df[h, :, cols].astype(BF)
            dy_copy(h, k).start()
            for d in order:
                dz_copy(h, k, 0, d).start()
        for h in range(2):
            for m in range(2):
                mo_own(h, k, m).start()
                for d in order:
                    mo_copy(h, k, m, d).start()

    def spread(k):
        for h in range(2):
            dy_copy(h, k).wait()
            for d in order:
                dz_copy(h, k, 1, d).start()

    def share(k):
        for h in range(2):
            for e in range(2):
                for d in order:
                    dz_copy(h, k, e, d).wait()
            dc_copy(h, k).start()

    def transpose_projector():
        for h in range(2):
            for b in range(R // 128):
                i = lax.broadcasted_iota(jnp.int32, (512, 512), 0)
                eye = (i == lax.broadcasted_iota(jnp.int32, (512, 512), 1)).astype(F32).astype(BF)
                pn[h, :, b * 128 : (b + 1) * 128] = lax.dot_general(
                    eye, pt[h, b * 128 : (b + 1) * 128, :], NT, preferred_element_type=F32
                ).astype(BF)

    def update(k):
        off, n = CHUNKS[k]
        cols = slice(off, off + n)
        for h in range(2):
            dc_copy(h, k).wait()
            for d in (2, 1, 3, 0):
                part = rows(lax.rem(gq[h] + d, 4) * ROWS, ROWS, ROWS)
                us[h, part, cols] = jnp.dot(pn[h, part, :], dr[h, :, cols], preferred_element_type=F32).astype(BF)
                if d:
                    u_copy(h, k, d).start()

    def weight(k):
        off, n = CHUNKS[k]
        cols = slice(off, off + n)
        for h in range(2):
            for d in (0, 1, 3, 2):
                j = lax.rem(gq[h] - d + 4, 4)
                here = at_cols(h, j, k)
                if d:
                    u_copy(h, k, d).wait()
                    u = ur[:, here]
                else:
                    u = us[h, rows(gq[h] * ROWS, ROWS, ROWS), cols]
                nw_ref[:, here] = (wl[:, here].astype(F32) - 0.25 * u.astype(F32)).astype(BF)

    last = K + 7
    for step in range(last):
        for s, run in reversed(list(enumerate((multiply, add_core, add_ring, adam, spread, share, update)))):
            if 0 <= step - s < K:
                run(step - s)
        if step == 1:
            transpose_projector()
    load_w.wait()
    for k in range(K):
        weight(k)
    for k in range(K):
        for h in range(2):
            for m in range(2):
                mo_own(h, k, m).wait()
                for d in order:
                    mo_copy(h, k, m, d).wait()


def shards(*inputs):
    inputs = [pltpu.with_memory_space_constraint(a, pltpu.HBM) for a in inputs]
    dma = pltpu.SemaphoreType.DMA
    hk = dma((2, K))
    hkd = dma((2, K, 3))
    return pl.pallas_call(
        kernel,
        out_shape=(
            pltpu.VMEM((ROWS, COLS), BF),
            pltpu.VMEM((MR, COLS), F32),
            pltpu.VMEM((MR, COLS), F32),
        ),
        in_specs=[pl.BlockSpec(memory_space=pl.ANY)] * 5,
        out_specs=[pl.BlockSpec(memory_space=pltpu.VMEM)] * 3,
        scratch_shapes=[
            pltpu.VMEM((ROWS, COLS), BF),
            pltpu.VMEM((ROWS, COLS), BF),
            pltpu.VMEM((ROWS, R), BF),
            pltpu.VMEM((2, 512, OWN), BF),
            pltpu.VMEM((2, R, 512), BF),
            pltpu.VMEM((2, 512, R), BF),
            pltpu.VMEM((2, 384, OWN), F32),
            pltpu.VMEM((2, 384, OWN), BF),
            pltpu.VMEM((2, 384, OWN), BF),
            pltpu.VMEM((2, 384, OWN), BF),
            pltpu.VMEM((2, 3, 96, OWN), BF),
            pltpu.VMEM((2, 48, OWN), F32),
            pltpu.VMEM((2, 48, OWN), BF),
            pltpu.VMEM((2, 48, OWN), BF),
            pltpu.VMEM((2, 2, 4, MR, OWN), F32),
            pltpu.VMEM((2, 2, 4, MR, OWN), F32),
            pltpu.VMEM((2, 48, OWN), F32),
            pltpu.VMEM((2, R, OWN), BF),
            pltpu.VMEM((2, 512, OWN), BF),
            pltpu.VMEM((ROWS, COLS), BF),
            pltpu.VMEM((4, 8, 128), F32),
            pltpu.VMEM((10, 8, 128), F32),
            pltpu.VMEM((8, 128), F32),
            dma((6,)), dma((2, 2)), dma((2, K, 3)),
            hkd, hkd,
            dma((2, 3)), dma((2, 3)),
            dma((2, 2, 3)), dma((2, 2, 3)),
            hk, hk,
            hkd, hkd,
            hk, hk,
            hk, hk,
            dma((2, K, 2, 3)), dma((2, K, 2, 3)),
            hk, hk,
            dma((2, K, 2, 3)), dma((2, K, 2, 3)),
            hkd, hkd,
            dma((10,)), dma((10,)),
        ],
        compiler_params=pltpu.CompilerParams(
            collective_id=0, has_side_effects=True, vmem_limit_bytes=50 * 1024 * 1024
        ),
        cost_estimate=pl.CostEstimate(flops=4 * ROWS * R * COLS, bytes_accessed=7_000_000, transcendentals=86016),
    )(*inputs)


def solution(mesh):
    split = P("fsdp", "mat")
    return jax.shard_map(
        shards,
        mesh=mesh,
        in_specs=(split, split, P("fsdp", None), split, split),
        out_specs=(split, split, split),
        check_vma=False,
    )
```
